32 devices in a mesh: dp: 16 (over z, y, x), tensor: 2 (over core).
Axes of the slice: x: 2, y: 2, z: 4, core: 2. Of those that a mesh axis runs over, the one named last changes fastest.
Arguments:
- tokens: bfloat16 [4096, 768], P(('dp', 'tensor')), may hold values from -6 to 6
- bounds: int32 [16, 5], P('dp'), may hold values from 0 to 256, as said below
- w_qkv: bfloat16 [3, 768, 768], P(None, None, 'tensor'), may hold values from -0.21875 to 0.21875
- b_qkv: bfloat16 [3, 768], P(None, 'tensor'), may hold values from -4 to 4
- w_dense: bfloat16 [768, 768], P('tensor'), may hold values from -0.875 to 0.875
- b_dense: bfloat16 [768], replicated, may hold values from -4 to 4
- w_up: bfloat16 [768, 3072], P(None, 'tensor'), may hold values from -0.21875 to 0.21875
- b_up: bfloat16 [3072], P('tensor'), may hold values from -6 to 6
- w_down: bfloat16 [3072, 768], P('tensor'), may hold values from -0.109375 to 0.109375
- b_down: bfloat16 [768], replicated, may hold values from -4 to 4
- norm1_gain: bfloat16 [768], replicated, may hold values from 0.099609375 to 1.8984375
- norm1_shift: bfloat16 [768], replicated, may hold values from -4 to 4
- norm2_gain: bfloat16 [768], replicated, may hold values from 0.099609375 to 1.8984375
- norm2_shift: bfloat16 [768], replicated, may hold values from -4 to 4
- cotangent: bfloat16 [4096, 768], P(('dp', 'tensor')), may hold values from -6 to 6
Outputs:
- output: bfloat16 [4096, 768], P(('dp', 'tensor'))
- grad_input: bfloat16 [4096, 768], P(('dp', 'tensor'))
- grad_qkv: float32 [3, 768, 768], P(None, 'dp', 'tensor')
- grad_qkv_bias: float32 [3, 768], P(None, 'tensor')
- grad_dense: float32 [768, 768], P('tensor', 'dp')
- grad_dense_bias: float32 [768], replicated
- grad_up: float32 [768, 3072], P('dp', 'tensor')
- grad_up_bias: float32 [3072], P('tensor')
- grad_down: float32 [3072, 768], P('tensor', 'dp')
- grad_down_bias: float32 [768], replicated
- grad_norm1_gain: float32 [768], replicated
- grad_norm1_shift: float32 [768], replicated
- grad_norm2_gain: float32 [768], replicated
- grad_norm2_shift: float32 [768], replicated
The draws below stay inside these ranges and needn't reach their ends.
Inputs may be any that keep to these rules, and one draw needn't show every extreme that they name: `bounds`: each row starts with 0 and never falls; each rise is 0 or at least 64; the first rise is at least 129; the last entry is the group's used slots, and some group uses all 256.
All inputs are finite; a program needn't handle non-finite values.
Results may differ from the reference program's by a relative error of at most 0.0095.
Values may be sent and summed in bfloat16 or wider, within the bound.
A program may use at most 128 MiB of HBM per device.

```python
import math
import jax
import jax.numpy as jnp
from jax import lax

D = 768
HEADS = 12
HEAD = 64
FF = 3072
ROT = 16
TOK_DEV = 256
MIN_LEN = 64
LEAD = 129
SLOTS = 4
TOKENS = 4096
N_DP = 16


def draw_bounds(key, part):
    key = jax.random.fold_in(key, 7)
    keys = jax.random.split(key, SLOTS + 3)
    used = TOK_DEV - jax.random.randint(keys[0], (N_DP,), 0, TOK_DEV - LEAD + 1)
    fullest = jax.random.randint(keys[1], (), 0, N_DP)
    used = jnp.where(jnp.arange(N_DP) == fullest, TOK_DEV, used)
    first = LEAD + jax.random.randint(keys[2], (N_DP,), 0, used - LEAD + 1)
    first = jnp.where(used - first < MIN_LEN, used, first)
    columns = [jnp.zeros((N_DP,), jnp.int32), first.astype(jnp.int32)]
    edge = first
    for slot in range(2, SLOTS + 1):
        left = used - edge
        if slot == SLOTS:
            take = left
        else:
            take = MIN_LEN + jax.random.randint(keys[slot + 1], (N_DP,), 0, jnp.maximum(left - MIN_LEN + 1, 1))
            take = jnp.where(left - take < MIN_LEN, left, take)
        edge = edge + take
        columns.append(edge.astype(jnp.int32))
    return jnp.stack(columns, 1).astype(jnp.int32)


def block_levels(own_key, extent, cuts, least, largest):
    level = 1.0
    for dim, shards_of in cuts:
        draws = jax.random.uniform(jax.random.fold_in(jax.random.fold_in(own_key, 6), dim), (shards_of,), jnp.float32, least / len(cuts), largest / len(cuts))
        level = level * jnp.repeat(jnp.exp(draws), extent[dim] // shards_of).reshape((-1,) + (1,) * (len(extent) - 1 - dim))
    return level


def centred(key, dims, width, limit, pieces=(), kind=jnp.bfloat16):
    array = width * jax.random.normal(key, dims, jnp.float32)
    if pieces:
        array = array * block_levels(key, dims, pieces, -0.22, 0.18)
    return jnp.clip(array, -limit, limit).astype(kind)


def setup_inputs(seed: int = 0) -> dict:
    splits = jax.random.split(jax.random.key(seed), 16)
    return {
        "tokens": centred(splits[0], (TOKENS, D), 1.0, 6.0, ((0, 32),)),
        "bounds": draw_bounds(jax.random.fold_in(splits[15], 71), 0),
        "w_qkv": centred(splits[2], (3, D, D), D ** -0.5, 0.21875, ((2, 2),)),
        "b_qkv": centred(splits[3], (3, D), 0.3, 4.0, ((1, 2),)),
        "w_dense": centred(splits[4], (D, D), (D // 16) ** -0.5, 0.875, ((0, 2),)),
        "b_dense": centred(splits[5], (D,), 0.3, 4.0),
        "w_up": centred(splits[6], (D, FF), D ** -0.5, 0.21875, ((1, 2),)),
        "b_up": centred(splits[7], (FF,), 0.5, 6.0, ((0, 2),)),
        "w_down": centred(splits[8], (FF, D), FF ** -0.5, 0.109375, ((0, 2),)),
        "b_down": centred(splits[9], (D,), 0.3, 4.0),
        "norm1_gain": jnp.clip(1.0 + 0.18 * jax.random.normal(splits[10], (D,), jnp.float32), 0.099609375, 1.8984375).astype(jnp.bfloat16),
        "norm1_shift": centred(splits[11], (D,), 0.3, 4.0),
        "norm2_gain": jnp.clip(1.0 + 0.18 * jax.random.normal(splits[12], (D,), jnp.float32), 0.099609375, 1.8984375).astype(jnp.bfloat16),
        "norm2_shift": centred(splits[13], (D,), 0.3, 4.0),
        "cotangent": centred(splits[14], (TOKENS, D), 1.0, 6.0, ((0, 32),)),
    }


HIGH = lax.Precision.HIGHEST
EPS = 1e-05

@jax.custom_vjp
def low(v):
    return lax.optimization_barrier(v.astype(jnp.bfloat16)).astype(jnp.float32)

@jax.custom_vjp
def low_back(v):
    return v

def low_keep(v):
    return (low(v), None)

def low_pass(kept, grad):
    return (grad,)

def back_keep(v):
    return (v, None)

def back_low(kept, grad):
    return (low(grad),)
low.defvjp(low_keep, low_pass)
low_back.defvjp(back_keep, back_low)

def both_ways(v):
    return low_back(low(v))

def normalize(v, gain, shift):
    center = v - lax.optimization_barrier(jnp.mean(v, -1, keepdims=True))
    spread = lax.optimization_barrier(jnp.mean(center * center, -1, keepdims=True))
    return center * lax.rsqrt(spread + EPS) * gain + shift

def turn_half(v):
    half = ROT // 2
    return jnp.concatenate([-v[..., half:ROT], v[..., :half]], -1)

def rotary(v, cosine, sine):
    part = v[..., :ROT]
    return jnp.concatenate([part * cosine + turn_half(part) * sine, v[..., ROT:]], -1)

def layout(bounds_row):
    steps = jnp.arange(TOK_DEV, dtype=jnp.int32)
    segment = lax.optimization_barrier(jnp.sum((steps[:, None] >= bounds_row[None, 1:]).astype(jnp.int32), 1))
    slot_ids = jnp.arange(SLOTS + 1, dtype=jnp.int32)
    start = lax.optimization_barrier(jnp.sum(jnp.where(slot_ids[None, :] == segment[:, None], bounds_row[None, :], 0), 1))
    place = (steps - start).astype(jnp.float32)
    inverse = 10000.0 ** (-jnp.arange(0, ROT, 2).astype(jnp.float32) / ROT)
    angle = place[:, None] * inverse[None, :]
    angle = jnp.concatenate([angle, angle], -1)[:, None, :]
    allowed = (segment[:, None] == segment[None, :]) & (steps[None, :] <= steps[:, None])
    return (jnp.cos(angle), jnp.sin(angle), allowed)

def attend(query, key, value, allowed):
    raw = low_back(jnp.einsum('qhe,khe->hqk', query, key, precision=HIGH))
    scores = jnp.where(allowed[None], raw * (1.0 / math.sqrt(HEAD)), -1e+30)
    top = lax.optimization_barrier(jnp.max(scores, -1, keepdims=True))
    weights = jnp.exp(scores - top)
    probs = low(weights / lax.optimization_barrier(jnp.sum(weights, -1, keepdims=True)))
    return jnp.einsum('hqk,khe->qhe', probs, value, precision=HIGH)

def group_forward(params, rows, bounds_rows):
    w_qkv, b_qkv, w_dense, b_dense, w_up, b_up, w_down, b_down, gain_one, shift_one, gain_two, shift_two = params
    group = rows.shape[0]
    first = low(normalize(rows, gain_one, shift_one))
    second = low(normalize(rows, gain_two, shift_two))
    project = jnp.einsum('gtd,cde->cgte', first, w_qkv, precision=HIGH) + b_qkv[:, None, None, :]
    project = low_back(project)
    split = project.reshape(3, group, TOK_DEV, HEADS, HEAD)
    cosine, sine, allowed = jax.vmap(layout)(bounds_rows)
    query = low(rotary(split[0], cosine, sine))
    key = low(rotary(split[1], cosine, sine))
    value = low(split[2])
    mixed = jax.vmap(attend)(query, key, value, allowed)
    mixed = both_ways(mixed.reshape(group, TOK_DEV, D))
    attn_out = jnp.einsum('gtd,de->gte', mixed, w_dense, precision=HIGH)
    inner = low_back(jnp.einsum('gtd,df->gtf', second, w_up, precision=HIGH) + b_up)
    active = low(jax.nn.gelu(inner, approximate=False))
    mlp_out = jnp.einsum('gtf,fd->gtd', active, w_down, precision=HIGH)
    return rows + (attn_out + mlp_out) + (b_dense + b_down)

def reference(tokens, bounds, w_qkv, b_qkv, w_dense, b_dense, w_up, b_up, w_down, b_down, norm1_gain, norm1_shift, norm2_gain, norm2_shift, cotangent):
    per = math.gcd(N_DP, 8)
    params = tuple((p.astype(jnp.float32) for p in (w_qkv, b_qkv, w_dense, b_dense, w_up, b_up, w_down, b_down, norm1_gain, norm1_shift, norm2_gain, norm2_shift)))
    rows = tokens.astype(jnp.float32).reshape(N_DP // per, per, TOK_DEV, D)
    bounds_groups = bounds.astype(jnp.int32).reshape(N_DP // per, per, SLOTS + 1)
    back = cotangent.astype(jnp.float32).reshape(N_DP // per, per, TOK_DEV, D)

    def whole(params, rows):

        def step(item):
            return group_forward(params, item[0], item[1])
        return lax.map(jax.checkpoint(step), (rows, bounds_groups))
    out, pullback = jax.vjp(whole, params, rows)
    grads, grad_rows = pullback(back)
    g_qkv, g_qkv_b, g_dense, g_dense_b, g_up, g_up_b, g_down, g_down_b, g_gain1, g_shift1, g_gain2, g_shift2 = grads
    return (out.reshape(TOKENS, D).astype(jnp.bfloat16), grad_rows.reshape(TOKENS, D).astype(jnp.bfloat16), g_qkv, g_qkv_b, g_dense, g_dense_b, g_up, g_up_b, g_down, g_down_b, g_gain1, g_shift1, g_gain2, g_shift2)
```

```python
import functools
import math

import jax
import jax.numpy as jnp
from jax import lax
from jax.experimental import pallas as pl
from jax.experimental.pallas import tpu as pltpu
from jax.sharding import PartitionSpec as P

MESH = pl.DeviceIdType.MESH
WIDE = 128
LAG = 2
ROWS_DP = 24
ROWS_ALL = 32

D = 768
HEAD = 64
ROT = 16


EPS = 1e-05


def normalize_rows(rows, gain, shift):
    center = rows - jnp.mean(rows, -1, keepdims=True)
    spread = jnp.mean(center * center, -1, keepdims=True)
    scaler = lax.rsqrt(spread + EPS)
    normal = center * scaler
    return (normal * gain + shift, normal, scaler)


def norm_back(grad_out, normal, scaler, gain):
    scaled = grad_out * gain
    inner_mean = jnp.mean(scaled, -1, keepdims=True)
    cross_mean = jnp.mean(scaled * normal, -1, keepdims=True)
    into = scaler * (scaled - inner_mean - normal * cross_mean)
    return (into, jnp.sum(grad_out * normal, 0), jnp.sum(grad_out, 0))


def turn_half(v):
    half = ROT // 2
    return jnp.concatenate([-v[..., half:ROT], v[..., :half]], -1)


def unturn_half(v):
    half = ROT // 2
    return jnp.concatenate([v[..., half:ROT], -v[..., :half]], -1)


def rotary(v, cosine, sine):
    part = v[..., :ROT]
    return jnp.concatenate([part * cosine + turn_half(part) * sine, v[..., ROT:]], -1)


def unrotary(grad, cosine, sine):
    part = grad[..., :ROT]
    return jnp.concatenate([part * cosine + unturn_half(part * sine), grad[..., ROT:]], -1)


def layout(bounds_row, count):
    slot_count = bounds_row.shape[0]
    steps = jnp.arange(count, dtype=jnp.int32)
    segment = jnp.sum((steps[:, None] >= bounds_row[None, 1:]).astype(jnp.int32), 1)
    slot_ids = jnp.arange(slot_count, dtype=jnp.int32)
    start = jnp.sum(jnp.where(slot_ids[None, :] == segment[:, None], bounds_row[None, :], 0), 1)
    place = (steps - start).astype(jnp.float32)
    inverse = 10000.0 ** (-jnp.arange(0, ROT, 2).astype(jnp.float32) / ROT)
    angle = place[:, None] * inverse[None, :]
    angle = jnp.concatenate([angle, angle], -1)[:, None, :]
    allowed = (segment[:, None] == segment[None, :]) & (steps[None, :] <= steps[:, None])
    return (jnp.cos(angle), jnp.sin(angle), allowed)


def gelu_exact(v):
    return jax.nn.gelu(v, approximate=False)


def bit_orders(steps):
    plain = list(range(steps))
    other = [1, 0] + plain[2:] if steps > 1 else plain
    return plain, other


def place_rows(left, dp_count, share, padded, order):
    count = left.shape[0]
    steps = len(order)
    rows = left.T.reshape(dp_count, share, count)
    if padded != share:
        rows = jnp.pad(rows, ((0, 0), (0, padded - share), (0, 0)))
    rows = rows.reshape((2,) * steps + (padded, count))
    rows = rows.transpose([steps - 1 - b for b in order] + [steps, steps + 1])
    return rows.reshape(dp_count * padded, count)


def reduce_kernel(plan, orders, dp_count, padded, *refs):
    lefts, rights = refs[:6], refs[6:10]
    vec_ref, out_ref, vec_out = refs[10:13]
    grid, landed, vec_acc, vec_got = refs[13:17]
    send_sem, recv_sem, vec_send, vec_recv = refs[17:]
    steps = len(orders[0])
    me = lax.axis_index("dp")
    side = lax.axis_index("tensor")
    bits = [(me // (1 << b)) % 2 for b in range(steps)]
    mates = [me + (1 - 2 * bits[b]) * (1 << b) for b in range(steps)]

    barrier = pltpu.get_barrier_semaphore()
    for mate in mates:
        pl.semaphore_signal(barrier, inc=1, device_id=(mate, side), device_id_type=MESH)
    pl.semaphore_signal(barrier, inc=1, device_id=(me, 1 - side), device_id_type=MESH)
    pl.semaphore_wait(barrier, steps + 1)

    def span(chunk, step):
        order = orders[chunk % 2]
        start = 0
        for s in range(step):
            start = start + bits[order[s]] * ((dp_count >> (s + 1)) * padded)
        return start, (dp_count >> (step + 1)) * padded

    def copy(chunk, step):
        order = orders[chunk % 2]
        start, half = span(chunk, step)
        away = pl.multiple_of(start + (1 - bits[order[step]]) * half, 16)
        offset = (dp_count - (dp_count >> step)) * padded
        return pltpu.make_async_remote_copy(
            src_ref=grid.at[chunk, pl.ds(away, half)],
            dst_ref=landed.at[chunk, pl.ds(offset, half)],
            send_sem=send_sem.at[chunk, step],
            recv_sem=recv_sem.at[chunk, step],
            device_id=(mates[order[step]], side),
            device_id_type=MESH,
        )

    def absorb(chunk, step):
        order = orders[chunk % 2]
        start, half = span(chunk, step)
        copy(chunk, step).wait_recv()
        keep = pl.ds(pl.multiple_of(start + bits[order[step]] * half, 16), half)
        offset = (dp_count - (dp_count >> step)) * padded
        total = grid[chunk, keep].astype(jnp.float32) + landed[chunk, pl.ds(offset, half)].astype(
            jnp.float32
        )
        if step == steps - 1:
            out_ref[chunk] = total
        else:
            grid[chunk, keep] = total.astype(jnp.bfloat16)

    def produce(chunk):
        which, right, column = plan[chunk]
        grid[chunk] = jnp.dot(
            lefts[2 * which + chunk % 2][...],
            rights[right][:, pl.ds(column, WIDE)],
            preferred_element_type=jnp.float32,
        ).astype(jnp.bfloat16)

    def vec_copy(step):
        if step == 0:
            rows, target = pl.ds(ROWS_DP, ROWS_ALL), (me, 1 - side)
        else:
            rows, target = pl.ds(0, ROWS_DP + ROWS_ALL), (mates[step - 1], side)
        return pltpu.make_async_remote_copy(
            src_ref=vec_acc.at[step, rows],
            dst_ref=vec_got.at[step, rows],
            send_sem=vec_send.at[step],
            recv_sem=vec_recv.at[step],
            device_id=target,
            device_id_type=MESH,
        )

    def vec_step(step):
        if step == 0:
            vec_acc[0] = vec_ref[...]
        else:
            vec_copy(step - 1).wait_recv()
            if step == 1:
                vec_acc[1, :ROWS_DP] = vec_acc[0, :ROWS_DP]
                vec_acc[1, ROWS_DP:] = vec_acc[0, ROWS_DP:] + vec_got[0, ROWS_DP:]
            elif step <= steps:
                vec_acc[step] = vec_acc[step - 1] + vec_got[step - 1]
            else:
                vec_out[...] = vec_acc[step - 1] + vec_got[step - 1]
        if step <= steps:
            vec_copy(step).start()

    chunks = len(plan)
    ticks = chunks + LAG * steps
    for tick in range(ticks):
        for step in range(steps, -1, -1):
            chunk = tick - LAG * step
            if 0 <= chunk < chunks:
                if step > 0:
                    absorb(chunk, step - 1)
                else:
                    produce(chunk)
                if step < steps:
                    copy(chunk, step).start()
        if tick % 3 == 0 and tick // 3 <= steps + 1:
            vec_step(tick // 3)
    for chunk in range(chunks):
        for step in range(steps):
            copy(chunk, step).wait_send()
    for step in range(steps + 1):
        vec_copy(step).wait_send()


def reduce_grads(first, second, back, grad_project, mixed, grad_inner, active, vec_dp, vec_all):
    f32 = jnp.float32
    bf16 = jnp.bfloat16
    dp_count = lax.axis_size("dp")
    steps = dp_count.bit_length() - 1
    share = D // dp_count
    padded = -(-share // 16) * 16
    orders = bit_orders(steps)
    lefts = [
        place_rows(left, dp_count, share, padded, order)
        for left in (second, back, first)
        for order in orders
    ]
    rights = (grad_inner, active, grad_project, mixed)
    plan = []
    for which, right in ((0, 0), (1, 1), (2, 2), (1, 3)):
        plan += [(which, right, c) for c in range(0, rights[right].shape[1], WIDE)]
    flat_dp = jnp.concatenate([v.reshape(-1) for v in vec_dp])
    flat_all = jnp.concatenate([v.reshape(-1) for v in vec_all])
    vec = jnp.concatenate(
        [
            jnp.pad(flat_dp, (0, ROWS_DP * 128 - flat_dp.shape[0])),
            jnp.pad(flat_all, (0, ROWS_ALL * 128 - flat_all.shape[0])),
        ]
    ).reshape(ROWS_DP + ROWS_ALL, 128)
    chunks = len(plan)
    whole = pl.BlockSpec(memory_space=pltpu.VMEM)
    out, vec = pl.pallas_call(
        functools.partial(reduce_kernel, plan, orders, dp_count, padded),
        out_shape=(
            jax.ShapeDtypeStruct((chunks, padded, WIDE), f32),
            jax.ShapeDtypeStruct((ROWS_DP + ROWS_ALL, 128), f32),
        ),
        in_specs=[whole] * 11,
        out_specs=(whole, whole),
        scratch_shapes=[
            pltpu.VMEM((chunks, dp_count * padded, WIDE), bf16),
            pltpu.VMEM((chunks, (dp_count - 1) * padded, WIDE), bf16),
            pltpu.VMEM((steps + 1, ROWS_DP + ROWS_ALL, 128), f32),
            pltpu.VMEM((steps + 1, ROWS_DP + ROWS_ALL, 128), f32),
            pltpu.SemaphoreType.DMA((chunks, steps)),
            pltpu.SemaphoreType.DMA((chunks, steps)),
            pltpu.SemaphoreType.DMA((steps + 1,)),
            pltpu.SemaphoreType.DMA((steps + 1,)),
        ],
        compiler_params=pltpu.CompilerParams(
            collective_id=0, has_side_effects=True, vmem_limit_bytes=60 * 1024 * 1024
        ),
    )(*lefts, *rights, vec)
    out = out[:, :share]
    pieces = []
    at = 0
    for right in rights:
        number = right.shape[1] // WIDE
        pieces.append(out[at : at + number])
        at += number
    up, down, qkv, dense = pieces
    shard_up = up.transpose(1, 0, 2).reshape(share, -1)
    shard_down = down.transpose(0, 2, 1).reshape(-1, share)
    shard_dense = dense.transpose(0, 2, 1).reshape(-1, share)
    each = qkv.shape[0] // 3
    shard_qkv = qkv.reshape(3, each, share, WIDE).transpose(0, 2, 1, 3).reshape(3, share, -1)
    flat = vec.reshape(-1)
    results = []
    at = 0
    for v in vec_dp:
        results.append(flat[at : at + v.size].reshape(v.shape))
        at += v.size
    at = ROWS_DP * 128
    for v in vec_all:
        results.append(flat[at : at + v.size].reshape(v.shape))
        at += v.size
    return shard_up, shard_down, shard_qkv, shard_dense, results


def on_device(
    tokens,
    bounds,
    w_qkv,
    b_qkv,
    w_dense,
    b_dense,
    w_up,
    b_up,
    w_down,
    b_down,
    norm1_gain,
    norm1_shift,
    norm2_gain,
    norm2_shift,
    cotangent,
):
    f32 = jnp.float32
    bf16 = jnp.bfloat16
    scale = 1.0 / math.sqrt(HEAD)
    rows = tokens.astype(f32)
    gain_one = norm1_gain.astype(f32)
    gain_two = norm2_gain.astype(f32)
    first_own, normal_one, scaler_one = normalize_rows(rows, gain_one, norm1_shift.astype(f32))
    second_own, normal_two, scaler_two = normalize_rows(rows, gain_two, norm2_shift.astype(f32))
    first, second = (
        lax.all_gather(first_own.astype(bf16), "tensor", axis=0, tiled=True),
        lax.all_gather(second_own.astype(bf16), "tensor", axis=0, tiled=True),
    )
    count = first.shape[0]
    width = w_qkv.shape[2]
    heads = width // HEAD
    cosine, sine, allowed = layout(bounds[0], count)
    project = (
        jnp.einsum("td,cde->cte", first, w_qkv, preferred_element_type=f32)
        + b_qkv.astype(f32)[:, None, :]
    )
    split = project.reshape(3, count, heads, HEAD)
    query = rotary(split[0], cosine, sine).astype(bf16)
    key = rotary(split[1], cosine, sine).astype(bf16)
    value = split[2].astype(bf16)
    raw = jnp.einsum("qhe,khe->hqk", query, key, preferred_element_type=f32)
    scaled = jnp.where(allowed[None], raw * scale, -1e30)
    top = jnp.max(scaled, -1, keepdims=True)
    weights = jnp.exp(scaled - top)
    total = jnp.sum(weights, -1, keepdims=True)
    log_total = top + jnp.log(total)
    probs = weights / total
    mixed = jnp.einsum("hqk,khe->qhe", probs.astype(bf16), value, preferred_element_type=f32)
    mixed = mixed.astype(bf16).reshape(count, width)
    inner = jnp.dot(second, w_up, preferred_element_type=f32) + b_up.astype(f32)
    active = gelu_exact(inner).astype(bf16)
    summed = lax.psum_scatter(
        (
            jnp.dot(mixed, w_dense, preferred_element_type=f32)
            + jnp.dot(active, w_down, preferred_element_type=f32)
        ).astype(jnp.bfloat16),
        "tensor",
        scatter_dimension=0,
        tiled=True,
    ).astype(jnp.float32)
    output = (rows + summed + (b_dense.astype(f32) + b_down.astype(f32))).astype(bf16)
    back = lax.all_gather(cotangent, "tensor", axis=0, tiled=True)
    grad_active = jnp.einsum("td,fd->tf", back, w_down, preferred_element_type=f32)
    grad_inner = jax.vjp(gelu_exact, inner)[1](grad_active)[0].astype(bf16)
    grad_up_b = jnp.sum(grad_inner.astype(f32), 0)
    part_second = jnp.einsum("tf,df->td", grad_inner, w_up, preferred_element_type=f32)
    grad_mixed = jnp.einsum("td,ed->te", back, w_dense, preferred_element_type=f32)
    grad_mixed = grad_mixed.astype(bf16).reshape(count, heads, HEAD)
    again = jnp.exp(scaled - log_total)
    grad_probs = jnp.einsum("qhe,khe->hqk", grad_mixed, value, preferred_element_type=f32)
    inner_sum = jnp.sum(grad_probs * again, -1, keepdims=True)
    grad_raw = (again * (grad_probs - inner_sum) * scale).astype(bf16)
    grad_query = jnp.einsum("hqk,khe->qhe", grad_raw, key, preferred_element_type=f32)
    grad_key = jnp.einsum("hqk,qhe->khe", grad_raw, query, preferred_element_type=f32)
    grad_value = jnp.einsum(
        "hqk,qhe->khe", again.astype(bf16), grad_mixed, preferred_element_type=f32
    )
    grad_project = jnp.stack(
        [unrotary(grad_query, cosine, sine), unrotary(grad_key, cosine, sine), grad_value]
    )
    grad_project = grad_project.reshape(3, count, width).astype(bf16)
    grad_qkv_b = jnp.sum(grad_project.astype(f32), 1)
    part_first = jnp.einsum("cte,cde->td", grad_project, w_qkv, preferred_element_type=f32)
    grad_first, grad_second = (
        lax.psum_scatter(
            part_first.astype(jnp.bfloat16), "tensor", scatter_dimension=0, tiled=True
        ).astype(jnp.float32),
        lax.psum_scatter(
            part_second.astype(jnp.bfloat16), "tensor", scatter_dimension=0, tiled=True
        ).astype(jnp.float32),
    )
    back_own = cotangent.astype(f32)
    into_one, gain_grad_one, shift_grad_one = norm_back(
        grad_first, normal_one, scaler_one, gain_one
    )
    into_two, gain_grad_two, shift_grad_two = norm_back(
        grad_second, normal_two, scaler_two, gain_two
    )
    grad_input = (back_own + into_one + into_two).astype(bf16)
    shard_up, shard_down, shard_qkv, shard_dense, vectors = reduce_grads(
        first,
        second,
        back,
        grad_project.transpose(1, 0, 2).reshape(count, 3 * width),
        mixed,
        grad_inner,
        active,
        (grad_qkv_b, grad_up_b),
        (gain_grad_one, shift_grad_one, gain_grad_two, shift_grad_two, jnp.sum(back_own, 0)),
    )
    sum_qkv_b, sum_up_b = vectors[:2]
    gain_sum_one, shift_sum_one, gain_sum_two, shift_sum_two, bias_sum = vectors[2:]
    return (
        output,
        grad_input,
        shard_qkv,
        sum_qkv_b,
        shard_dense,
        bias_sum,
        shard_up,
        sum_up_b,
        shard_down,
        bias_sum,
        gain_sum_one,
        shift_sum_one,
        gain_sum_two,
        shift_sum_two,
    )


def solution(mesh):
    return jax.shard_map(
        on_device,
        mesh=mesh,
        in_specs=(
            P(("dp", "tensor"), None),
            P("dp", None),
            P(None, None, "tensor"),
            P(None, "tensor"),
            P("tensor", None),
            P(),
            P(None, "tensor"),
            P("tensor"),
            P("tensor", None),
            P(),
            P(),
            P(),
            P(),
            P(),
            P(("dp", "tensor"), None),
        ),
        out_specs=(
            P(("dp", "tensor"), None),
            P(("dp", "tensor"), None),
            P(None, "dp", "tensor"),
            P(None, "tensor"),
            P("tensor", "dp"),
            P(),
            P("dp", "tensor"),
            P("tensor"),
            P("tensor", "dp"),
            P(),
            P(),
            P(),
            P(),
            P(),
        ),
        check_vma=False,
    )
```

```python
import functools
import math

import jax
import jax.numpy as jnp
from jax import lax
from jax.experimental import pallas as pl
from jax.experimental.pallas import tpu as pltpu
from jax.sharding import PartitionSpec as P

MESH = pl.DeviceIdType.MESH
WIDE = 128
LAG = 4
ROWS_DP = 24
ROWS_ALL = 32

D = 768
HEAD = 64
ROT = 16


EPS = 1e-05


def normalize_rows(rows, gain, shift):
    center = rows - jnp.mean(rows, -1, keepdims=True)
    spread = jnp.mean(center * center, -1, keepdims=True)
    scaler = lax.rsqrt(spread + EPS)
    normal = center * scaler
    return (normal * gain + shift, normal, scaler)


def norm_back(grad_out, normal, scaler, gain):
    scaled = grad_out * gain
    inner_mean = jnp.mean(scaled, -1, keepdims=True)
    cross_mean = jnp.mean(scaled * normal, -1, keepdims=True)
    into = scaler * (scaled - inner_mean - normal * cross_mean)
    return (into, jnp.sum(grad_out * normal, 0), jnp.sum(grad_out, 0))


def turn_half(v):
    half = ROT // 2
    return jnp.concatenate([-v[..., half:ROT], v[..., :half]], -1)


def unturn_half(v):
    half = ROT // 2
    return jnp.concatenate([v[..., half:ROT], -v[..., :half]], -1)


def rotary(v, cosine, sine):
    part = v[..., :ROT]
    return jnp.concatenate([part * cosine + turn_half(part) * sine, v[..., ROT:]], -1)


def unrotary(grad, cosine, sine):
    part = grad[..., :ROT]
    return jnp.concatenate([part * cosine + unturn_half(part * sine), grad[..., ROT:]], -1)


def layout(bounds_row, count):
    slot_count = bounds_row.shape[0]
    steps = jnp.arange(count, dtype=jnp.int32)
    segment = jnp.sum((steps[:, None] >= bounds_row[None, 1:]).astype(jnp.int32), 1)
    slot_ids = jnp.arange(slot_count, dtype=jnp.int32)
    start = jnp.sum(jnp.where(slot_ids[None, :] == segment[:, None], bounds_row[None, :], 0), 1)
    place = (steps - start).astype(jnp.float32)
    inverse = 10000.0 ** (-jnp.arange(0, ROT, 2).astype(jnp.float32) / ROT)
    angle = place[:, None] * inverse[None, :]
    angle = jnp.concatenate([angle, angle], -1)[:, None, :]
    allowed = (segment[:, None] == segment[None, :]) & (steps[None, :] <= steps[:, None])
    return (jnp.cos(angle), jnp.sin(angle), allowed)


def gelu_exact(v):
    return jax.nn.gelu(v, approximate=False)


def bit_orders(steps):
    plain = list(range(steps))
    other = [1, 0] + plain[2:] if steps > 1 else plain
    far = plain[2:] + plain[:2]
    return plain, other, far


def place_rows(left, dp_count, share, padded, order):
    count = left.shape[0]
    steps = len(order)
    rows = left.T.reshape(dp_count, share, count)
    if padded != share:
        rows = jnp.pad(rows, ((0, 0), (0, padded - share), (0, 0)))
    rows = rows.reshape((2,) * steps + (padded, count))
    rows = rows.transpose([steps - 1 - b for b in order] + [steps, steps + 1])
    return rows.reshape(dp_count * padded, count)


def reduce_kernel(plan, orders, dp_count, padded, *refs):
    lefts, rights = refs[:3], refs[3:7]
    vec_ref, out_ref, vec_out = refs[7:10]
    grid, landed, vec_acc, vec_got = refs[10:14]
    send_sem, recv_sem, vec_send, vec_recv = refs[14:]
    steps = len(orders[0])
    by_array = sorted(range(len(plan)), key=lambda chunk: plan[chunk][1:])
    slots = {chunk: slot for slot, chunk in enumerate(by_array)}
    me = lax.axis_index("dp")
    side = lax.axis_index("tensor")
    bits = [(me // (1 << b)) % 2 for b in range(steps)]
    mates = [me + (1 - 2 * bits[b]) * (1 << b) for b in range(steps)]

    barrier = pltpu.get_barrier_semaphore()
    for mate in mates:
        pl.semaphore_signal(barrier, inc=1, device_id=(mate, side), device_id_type=MESH)
    pl.semaphore_signal(barrier, inc=1, device_id=(me, 1 - side), device_id_type=MESH)
    pl.semaphore_wait(barrier, steps + 1)

    def span(chunk, step):
        order = orders[plan[chunk][0]]
        start = 0
        for s in range(step):
            start = start + bits[order[s]] * ((dp_count >> (s + 1)) * padded)
        return start, (dp_count >> (step + 1)) * padded

    def copy(chunk, step):
        order = orders[plan[chunk][0]]
        start, half = span(chunk, step)
        away = pl.multiple_of(start + (1 - bits[order[step]]) * half, 16)
        offset = (dp_count - (dp_count >> step)) * padded
        return pltpu.make_async_remote_copy(
            src_ref=grid.at[chunk, pl.ds(away, half)],
            dst_ref=landed.at[chunk, pl.ds(offset, half)],
            send_sem=send_sem.at[chunk, step],
            recv_sem=recv_sem.at[chunk, step],
            device_id=(mates[order[step]], side),
            device_id_type=MESH,
        )

    def absorb(chunk, step):
        order = orders[plan[chunk][0]]
        start, half = span(chunk, step)
        copy(chunk, step).wait_recv()
        keep = pl.ds(pl.multiple_of(start + bits[order[step]] * half, 16), half)
        offset = (dp_count - (dp_count >> step)) * padded
        total = grid[chunk, keep].astype(jnp.float32) + landed[chunk, pl.ds(offset, half)].astype(
            jnp.float32
        )
        if step == steps - 1:
            out_ref[slots[chunk]] = total
        else:
            grid[chunk, keep] = total.astype(jnp.bfloat16)

    def produce(chunk):
        which, right, column = plan[chunk]
        grid[chunk] = jnp.dot(
            lefts[which][...],
            rights[right][:, pl.ds(column, WIDE)],
            preferred_element_type=jnp.float32,
        ).astype(jnp.bfloat16)

    def vec_copy(step):
        if step == 0:
            rows, target = pl.ds(ROWS_DP, ROWS_ALL), (me, 1 - side)
        else:
            rows, target = pl.ds(0, ROWS_DP + ROWS_ALL), (mates[step - 1], side)
        return pltpu.make_async_remote_copy(
            src_ref=vec_acc.at[step, rows],
            dst_ref=vec_got.at[step, rows],
            send_sem=vec_send.at[step],
            recv_sem=vec_recv.at[step],
            device_id=target,
            device_id_type=MESH,
        )

    def vec_step(step):
        if step == 0:
            vec_acc[0] = vec_ref[...]
        else:
            vec_copy(step - 1).wait_recv()
            if step == 1:
                vec_acc[1, :ROWS_DP] = vec_acc[0, :ROWS_DP]
                vec_acc[1, ROWS_DP:] = vec_acc[0, ROWS_DP:] + vec_got[0, ROWS_DP:]
            elif step <= steps:
                vec_acc[step] = vec_acc[step - 1] + vec_got[step - 1]
            else:
                vec_out[...] = vec_acc[step - 1] + vec_got[step - 1]
        if step <= steps:
            vec_copy(step).start()

    chunks = len(plan)
    ticks = chunks + LAG * steps
    for tick in range(ticks):
        for step in range(steps, -1, -1):
            chunk = tick - LAG * step
            if 0 <= chunk < chunks:
                if step > 0:
                    absorb(chunk, step - 1)
                else:
                    produce(chunk)
                if step < steps:
                    copy(chunk, step).start()
        if tick % 3 == 0 and tick // 3 <= steps + 1:
            vec_step(tick // 3)
    for chunk in range(chunks):
        for step in range(steps):
            copy(chunk, step).wait_send()
    for step in range(steps + 1):
        vec_copy(step).wait_send()


def reduce_grads(first, second, back, grad_project, mixed, grad_inner, active, vec_dp, vec_all):
    f32 = jnp.float32
    bf16 = jnp.bfloat16
    dp_count = lax.axis_size("dp")
    steps = dp_count.bit_length() - 1
    share = D // dp_count
    padded = -(-share // 16) * 16
    orders = bit_orders(steps)
    lefts = [
        place_rows(left, dp_count, share, padded, orders[which])
        for which, left in enumerate((second, back, first))
    ]
    rights = (grad_inner, active, grad_project, mixed)
    plan = []
    for which, right in ((0, 0), (1, 1), (2, 2), (1, 3)):
        columns = range(0, rights[right].shape[1], WIDE)
        plan += [((i + 0.5) / len(columns), which, right, c) for i, c in enumerate(columns)]
    plan = [entry[1:] for entry in sorted(plan)]
    flat_dp = jnp.concatenate([v.reshape(-1) for v in vec_dp])
    flat_all = jnp.concatenate([v.reshape(-1) for v in vec_all])
    vec = jnp.concatenate(
        [
            jnp.pad(flat_dp, (0, ROWS_DP * 128 - flat_dp.shape[0])),
            jnp.pad(flat_all, (0, ROWS_ALL * 128 - flat_all.shape[0])),
        ]
    ).reshape(ROWS_DP + ROWS_ALL, 128)
    chunks = len(plan)
    whole = pl.BlockSpec(memory_space=pltpu.VMEM)
    out, vec = pl.pallas_call(
        functools.partial(reduce_kernel, plan, orders, dp_count, padded),
        out_shape=(
            jax.ShapeDtypeStruct((chunks, padded, WIDE), f32),
            jax.ShapeDtypeStruct((ROWS_DP + ROWS_ALL, 128), f32),
        ),
        in_specs=[whole] * 8,
        out_specs=(whole, whole),
        scratch_shapes=[
            pltpu.VMEM((chunks, dp_count * padded, WIDE), bf16),
            pltpu.VMEM((chunks, (dp_count - 1) * padded, WIDE), bf16),
            pltpu.VMEM((steps + 1, ROWS_DP + ROWS_ALL, 128), f32),
            pltpu.VMEM((steps + 1, ROWS_DP + ROWS_ALL, 128), f32),
            pltpu.SemaphoreType.DMA((chunks, steps)),
            pltpu.SemaphoreType.DMA((chunks, steps)),
            pltpu.SemaphoreType.DMA((steps + 1,)),
            pltpu.SemaphoreType.DMA((steps + 1,)),
        ],
        compiler_params=pltpu.CompilerParams(
            collective_id=0, has_side_effects=True, vmem_limit_bytes=60 * 1024 * 1024
        ),
    )(*lefts, *rights, vec)
    out = out[:, :share]
    pieces = []
    at = 0
    for right in rights:
        number = right.shape[1] // WIDE
        pieces.append(out[at : at + number])
        at += number
    up, down, qkv, dense = pieces
    shard_up = up.transpose(1, 0, 2).reshape(share, -1)
    shard_down = down.transpose(0, 2, 1).reshape(-1, share)
    shard_dense = dense.transpose(0, 2, 1).reshape(-1, share)
    each = qkv.shape[0] // 3
    shard_qkv = qkv.reshape(3, each, share, WIDE).transpose(0, 2, 1, 3).reshape(3, share, -1)
    flat = vec.reshape(-1)
    results = []
    at = 0
    for v in vec_dp:
        results.append(flat[at : at + v.size].reshape(v.shape))
        at += v.size
    at = ROWS_DP * 128
    for v in vec_all:
        results.append(flat[at : at + v.size].reshape(v.shape))
        at += v.size
    return shard_up, shard_down, shard_qkv, shard_dense, results


def pair_sum(part):
    mine = lax.axis_index("tensor")
    part = part.astype(jnp.bfloat16)
    half = part.shape[0] // 2
    away = lax.dynamic_slice_in_dim(part, (1 - mine) * half, half, 0)
    kept = lax.dynamic_slice_in_dim(part, mine * half, half, 0)
    got = lax.ppermute(away, "tensor", [(0, 1), (1, 0)])
    return kept.astype(jnp.float32) + got.astype(jnp.float32)


def on_device(
    tokens,
    bounds,
    w_qkv,
    b_qkv,
    w_dense,
    b_dense,
    w_up,
    b_up,
    w_down,
    b_down,
    norm1_gain,
    norm1_shift,
    norm2_gain,
    norm2_shift,
    cotangent,
):
    f32 = jnp.float32
    bf16 = jnp.bfloat16
    scale = 1.0 / math.sqrt(HEAD)
    rows = tokens.astype(f32)
    gain_one = norm1_gain.astype(f32)
    gain_two = norm2_gain.astype(f32)
    first_own, normal_one, scaler_one = normalize_rows(rows, gain_one, norm1_shift.astype(f32))
    second_own, normal_two, scaler_two = normalize_rows(rows, gain_two, norm2_shift.astype(f32))
    first, second = (
        lax.all_gather(first_own.astype(bf16), "tensor", axis=0, tiled=True),
        lax.all_gather(second_own.astype(bf16), "tensor", axis=0, tiled=True),
    )
    count = first.shape[0]
    width = w_qkv.shape[2]
    heads = width // HEAD
    cosine, sine, allowed = layout(bounds[0], count)
    project = (
        jnp.einsum("td,cde->cte", first, w_qkv, preferred_element_type=f32)
        + b_qkv.astype(f32)[:, None, :]
    )
    split = project.reshape(3, count, heads, HEAD)
    query = rotary(split[0], cosine, sine).astype(bf16)
    key = rotary(split[1], cosine, sine).astype(bf16)
    value = split[2].astype(bf16)
    raw = jnp.einsum("qhe,khe->hqk", query, key, preferred_element_type=f32)
    scaled = jnp.where(allowed[None], raw * scale, -1e30)
    top = jnp.max(scaled, -1, keepdims=True)
    weights = jnp.exp(scaled - top)
    total = jnp.sum(weights, -1, keepdims=True)
    log_total = top + jnp.log(total)
    probs = weights / total
    mixed = jnp.einsum("hqk,khe->qhe", probs.astype(bf16), value, preferred_element_type=f32)
    mixed = mixed.astype(bf16).reshape(count, width)
    inner = jnp.dot(second, w_up, preferred_element_type=f32) + b_up.astype(f32)
    active = gelu_exact(inner).astype(bf16)
    summed = pair_sum(
        jnp.dot(mixed, w_dense, preferred_element_type=f32)
        + jnp.dot(active, w_down, preferred_element_type=f32)
    )
    output = (rows + summed + (b_dense.astype(f32) + b_down.astype(f32))).astype(bf16)
    back = lax.all_gather(cotangent, "tensor", axis=0, tiled=True)
    grad_active = jnp.einsum("td,fd->tf", back, w_down, preferred_element_type=f32)
    grad_inner = jax.vjp(gelu_exact, inner)[1](grad_active)[0].astype(bf16)
    grad_up_b = jnp.sum(grad_inner.astype(f32), 0)
    part_second = jnp.einsum("tf,df->td", grad_inner, w_up, preferred_element_type=f32)
    grad_mixed = jnp.einsum("td,ed->te", back, w_dense, preferred_element_type=f32)
    grad_mixed = grad_mixed.astype(bf16).reshape(count, heads, HEAD)
    again = jnp.exp(scaled - log_total)
    grad_probs = jnp.einsum("qhe,khe->hqk", grad_mixed, value, preferred_element_type=f32)
    inner_sum = jnp.sum(grad_probs * again, -1, keepdims=True)
    grad_raw = (again * (grad_probs - inner_sum) * scale).astype(bf16)
    grad_query = jnp.einsum("hqk,khe->qhe", grad_raw, key, preferred_element_type=f32)
    grad_key = jnp.einsum("hqk,qhe->khe", grad_raw, query, preferred_element_type=f32)
    grad_value = jnp.einsum(
        "hqk,qhe->khe", again.astype(bf16), grad_mixed, preferred_element_type=f32
    )
    grad_project = jnp.stack(
        [unrotary(grad_query, cosine, sine), unrotary(grad_key, cosine, sine), grad_value]
    )
    grad_project = grad_project.reshape(3, count, width).astype(bf16)
    grad_qkv_b = jnp.sum(grad_project.astype(f32), 1)
    part_first = jnp.einsum("cte,cde->td", grad_project, w_qkv, preferred_element_type=f32)
    grad_first = pair_sum(part_first)
    grad_second = pair_sum(part_second)
    back_own = cotangent.astype(f32)
    into_one, gain_grad_one, shift_grad_one = norm_back(
        grad_first, normal_one, scaler_one, gain_one
    )
    into_two, gain_grad_two, shift_grad_two = norm_back(
        grad_second, normal_two, scaler_two, gain_two
    )
    grad_input = (back_own + into_one + into_two).astype(bf16)
    shard_up, shard_down, shard_qkv, shard_dense, vectors = reduce_grads(
        first,
        second,
        back,
        grad_project.transpose(1, 0, 2).reshape(count, 3 * width),
        mixed,
        grad_inner,
        active,
        (grad_qkv_b, grad_up_b),
        (gain_grad_one, shift_grad_one, gain_grad_two, shift_grad_two, jnp.sum(back_own, 0)),
    )
    sum_qkv_b, sum_up_b = vectors[:2]
    gain_sum_one, shift_sum_one, gain_sum_two, shift_sum_two, bias_sum = vectors[2:]
    return (
        output,
        grad_input,
        shard_qkv,
        sum_qkv_b,
        shard_dense,
        bias_sum,
        shard_up,
        sum_up_b,
        shard_down,
        bias_sum,
        gain_sum_one,
        shift_sum_one,
        gain_sum_two,
        shift_sum_two,
    )


def solution(mesh):
    return jax.shard_map(
        on_device,
        mesh=mesh,
        in_specs=(
            P(("dp", "tensor"), None),
            P("dp", None),
            P(None, None, "tensor"),
            P(None, "tensor"),
            P("tensor", None),
            P(),
            P(None, "tensor"),
            P("tensor"),
            P("tensor", None),
            P(),
            P(),
            P(),
            P(),
            P(),
            P(("dp", "tensor"), None),
        ),
        out_specs=(
            P(("dp", "tensor"), None),
            P(("dp", "tensor"), None),
            P(None, "dp", "tensor"),
            P(None, "tensor"),
            P("tensor", "dp"),
            P(),
            P("dp", "tensor"),
            P("tensor"),
            P("tensor", "dp"),
            P(),
            P(),
            P(),
            P(),
            P(),
        ),
        check_vma=False,
    )
```
